32 devices in a mesh: groups: 2 (over y), dp: 16 (over z, x, core).
Axes of the slice: x: 2, y: 2, z: 4, core: 2. Of those that a mesh axis runs over, the one named last changes fastest.
Arguments:
- query_states: bfloat16 [128, 128, 2048], P(('groups', 'dp')), parts along dimension 0, may hold values from -4.5 to 4.5
- key_states: bfloat16 [128, 128, 512], P(('groups', 'dp')), parts along dimension 0, may hold values from -4.5 to 4.5
- value_states: bfloat16 [128, 128, 512], P(('groups', 'dp')), parts along dimension 0, may hold values from -56 to 56
- out_weight: bfloat16 [2048, 2048], P('dp'), may hold values from -0.125 to 0.125
- token_ids: int32 [128, 128], P(('groups', 'dp')), parts along dimension 0, may hold values from 0 to 31999, as said below
- keep_flags: int32 [128], P(('groups', 'dp')), parts along dimension 0, may hold values from 0 to 1, as said below
- list_ids: int32 [128, 128], P(('groups', 'dp')), parts along dimension 0, may hold values from 0 to 1023, as said below
- owner_map: int32 [2048], P('groups'), parts along dimension 0, may hold values from 0 to 15, as said below
Outputs:
- doc_vectors: bfloat16 [96, 2048], P(('groups', 'dp')), parts along dimension 0
- token_vectors: bfloat16 [16384, 2048], P(('groups', 'dp')), parts along dimension 0
- token_keys: int32 [16384], P(('groups', 'dp')), parts along dimension 0
The draws below stay inside these ranges and needn't reach their ends.
There are 2 independent parts, one for each index of `groups`. The reference program is written for one: setup_inputs(seed, part) draws one part's arguments, and reference() takes and returns one part's arrays. A program takes and returns all parts, laid end to end along the dimension named above; an argument that names none is the same for every part. Nothing has to cross between parts.
Inputs may be any that keep to these rules, and one draw needn't show every extreme that they name: `token_ids`: in each document the ids are 0 exactly from its length on, and its length lies between 96 and 128. `keep_flags`: exactly 48 documents have the flag 1. `list_ids`: the tokens of the 4 documents of one index of dp name lists of any one owner between 16 and 48 times, exactly 48 times for some owner; over all 64 documents the lists of each owner are named exactly 512 times. `owner_map`: every owner holds exactly 64 lists.
All inputs are finite; a program needn't handle non-finite values.
Results may differ from the reference program's by a relative error of at most 0.0057.
Values may be sent and summed in bfloat16 or wider, within the bound.
A program may use at most 64 MiB of HBM per device.

```python
import math
import jax
import jax.numpy as jnp
from jax import lax

HEAD_DIM = 128
OUT_DIM = 2048
VOCAB = 32000
DOC_LEN = 128
DOCS_DEV = 4
LIST_DEV = 64
FEATURES = 2048
KV_FEATURES = 512
OWNERS = 16
DOCS = 64
KEPT = 48
KEPT_DEV = 3
LISTS = 1024
OWN_CAP = 512


def draw_query_states(key, part):
    shape = (DOCS, DOC_LEN, FEATURES)
    states = jnp.clip(jax.random.normal(jax.random.fold_in(key, 43), shape, jnp.float32), -4.0, 4.0)
    return states.astype(jnp.bfloat16)


def draw_key_states(key, part):
    shape = (DOCS, DOC_LEN, KV_FEATURES)
    states = jnp.clip(jax.random.normal(jax.random.fold_in(key, 45), shape, jnp.float32), -4.0, 4.0)
    return states.astype(jnp.bfloat16)


def draw_value_states(key, part):
    shape = (DOCS, DOC_LEN, KV_FEATURES)
    noise = jnp.clip(jax.random.normal(jax.random.fold_in(key, 51), shape, jnp.float32), -4.0, 4.0)
    states = noise
    return states.astype(jnp.bfloat16)


def draw_token_ids(key, part):
    lengths = jax.random.randint(jax.random.fold_in(key, 21), (DOCS,), 3 * DOC_LEN // 4, DOC_LEN + 1)
    lengths = lengths.at[0].set(3 * DOC_LEN // 4).at[1].set(DOC_LEN)
    codes = jax.random.randint(jax.random.fold_in(key, 22), (DOCS, DOC_LEN), 1, VOCAB)
    codes = codes.at[0, 0].set(VOCAB - 1)
    positions = jnp.arange(DOC_LEN)[None, :]
    return jnp.where(positions < lengths[:, None], codes, 0).astype(jnp.int32)


def draw_keep_flags(key, part):
    shuffled = jax.random.permutation(jax.random.fold_in(key, 11), DOCS)
    return (shuffled < KEPT).astype(jnp.int32)


def list_tables(key):
    base = jax.random.fold_in(key, 31)
    shuffled = jax.random.permutation(jax.random.fold_in(base, 1), LISTS)
    owner_table = shuffled % OWNERS
    inverse = jnp.argsort(shuffled)
    half = OWNERS // 2
    mean_load = DOCS_DEV * DOC_LEN // OWNERS
    moves = jax.random.randint(jax.random.fold_in(base, 2), (half,), 0, mean_load // 2 + 1)
    moves = moves.at[0].set(mean_load // 2)
    pairing = jax.random.permutation(jax.random.fold_in(base, 3), OWNERS)
    profile = jnp.zeros((OWNERS,), jnp.int32)
    profile = profile.at[pairing[:half]].set(mean_load + moves)
    profile = profile.at[pairing[half:]].set(mean_load - moves)
    offsets = jax.random.permutation(jax.random.fold_in(base, 4), OWNERS)
    device_keys = jax.random.split(jax.random.fold_in(base, 5), OWNERS)

    def device_owners(offset, device_key):
        counts = jnp.roll(profile, offset)
        sequence = jnp.repeat(jnp.arange(OWNERS, dtype=jnp.int32), counts, total_repeat_length=DOCS_DEV * DOC_LEN)
        return jax.random.permutation(device_key, sequence)
    owners = jax.vmap(device_owners)(offsets, device_keys).reshape(DOCS, DOC_LEN)
    picks = jax.random.randint(jax.random.fold_in(base, 6), (DOCS, DOC_LEN), 0, LIST_DEV)
    highest = shuffled[LISTS - 1]
    lowest = shuffled[0]
    first_rows = picks[:DOCS_DEV]
    first_rows = jnp.where(owners[:DOCS_DEV] == highest % OWNERS, highest // OWNERS, first_rows)
    second_rows = picks[DOCS_DEV:2 * DOCS_DEV]
    second_rows = jnp.where(owners[DOCS_DEV:2 * DOCS_DEV] == lowest % OWNERS, lowest // OWNERS, second_rows)
    picks = picks.at[:DOCS_DEV].set(first_rows).at[DOCS_DEV:2 * DOCS_DEV].set(second_rows)
    lists = inverse[owners + OWNERS * picks]
    return (owner_table, lists)


def draw_list_ids(key, part):
    return list_tables(key)[1].astype(jnp.int32)


def draw_owner_map(key, part):
    return list_tables(key)[0].astype(jnp.int32)


def block_scale(rng, dims, cuts, smallest, top_value):
    def one(dim, parts):
        steps = jax.random.uniform(jax.random.fold_in(jax.random.fold_in(rng, 6), dim), (parts,), jnp.float32, smallest / len(cuts), top_value / len(cuts))
        return jnp.repeat(jnp.exp(steps), dims[dim] // parts).reshape((-1,) + (1,) * (len(dims) - dim - 1))

    loudness = one(*cuts[0])
    for cut in cuts[1:]:
        loudness = loudness * one(*cut)
    return loudness


def normal_values(rng, extent, width, bound, shards=(), kind=jnp.bfloat16):
    loudness = block_scale(rng, extent, shards, -0.22, 0.18) if shards else 1.0
    values = jax.random.normal(rng, extent, jnp.float32) * width * loudness
    return jnp.minimum(jnp.maximum(values, -bound), bound).astype(kind)


def setup_inputs(seed: int = 0, part: int = 0) -> dict:
    keys = jax.random.split(jax.random.key(seed), 9)
    part_splits = jax.random.split(jax.random.fold_in(keys[8], part), 9)
    query_states = draw_query_states(jax.random.fold_in(jax.random.fold_in(keys[8], part), 71), part)
    key_states = draw_key_states(jax.random.fold_in(jax.random.fold_in(keys[8], part), 71), part)
    value_states = draw_value_states(jax.random.fold_in(jax.random.fold_in(keys[8], part), 71), part)
    out_weight = normal_values(keys[3], (FEATURES, OUT_DIM), FEATURES ** -0.5, 0.125, ((0, 16),))
    token_ids = draw_token_ids(jax.random.fold_in(jax.random.fold_in(keys[8], part), 71), part)
    keep_flags = draw_keep_flags(jax.random.fold_in(jax.random.fold_in(keys[8], part), 71), part)
    list_ids = draw_list_ids(jax.random.fold_in(jax.random.fold_in(keys[8], part), 71), part)
    owner_map = draw_owner_map(jax.random.fold_in(jax.random.fold_in(keys[8], part), 71), part)
    return dict(query_states=query_states, key_states=key_states, value_states=value_states, out_weight=out_weight, token_ids=token_ids, keep_flags=keep_flags, list_ids=list_ids, owner_map=owner_map)


def attend_one(inputs):
    query_doc, key_doc, value_doc, code_doc = inputs
    length, features = query_doc.shape
    kv_features = key_doc.shape[1]
    kv_count = kv_features // HEAD_DIM
    group_size = features // kv_features
    queries = query_doc.reshape(length, kv_count, group_size, HEAD_DIM).astype(jnp.float32)
    keys_split = key_doc.reshape(length, kv_count, HEAD_DIM).astype(jnp.float32)
    values_split = value_doc.reshape(length, kv_count, HEAD_DIM).astype(jnp.float32)
    scores = jnp.einsum('qhgd,shd->hgqs', queries, keys_split) / math.sqrt(HEAD_DIM)
    present = code_doc != 0
    scores = jnp.where(present[None, None, None, :], scores, -jnp.inf)
    row_max = lax.optimization_barrier(jnp.max(scores, axis=-1, keepdims=True))
    weights = jnp.exp(scores - row_max)
    weights = (weights / lax.optimization_barrier(jnp.sum(weights, axis=-1, keepdims=True))).astype(jnp.bfloat16)
    weights = lax.optimization_barrier(weights)
    attended = jnp.einsum('hgqs,shd->qhgd', weights.astype(jnp.float32), values_split).reshape(length, features).astype(jnp.bfloat16)
    attended = lax.optimization_barrier(attended)
    wide = attended.astype(jnp.float32)
    counts = jnp.sum(present.astype(jnp.float32))
    pooled_attended = lax.optimization_barrier(jnp.sum(jnp.where(present[:, None], wide, jnp.zeros_like(wide)), axis=0)) / counts
    return (attended, pooled_attended)

def normalize(values):
    return (values * lax.rsqrt(lax.optimization_barrier(jnp.mean(values * values, axis=-1, keepdims=True)) + 1e-06)).astype(jnp.bfloat16)

def reference(query_states, key_states, value_states, out_weight, token_ids, keep_flags, list_ids, owner_map):
    attended, pooled_attended = lax.map(attend_one, (query_states, key_states, value_states, token_ids))
    weight_wide = out_weight.astype(jnp.float32)

    def project_one(rows):
        projected = jnp.dot(rows.astype(jnp.float32), weight_wide, precision=lax.Precision.HIGHEST)
        return normalize(projected)
    unit_tokens = lax.map(project_one, attended)
    pooled = jnp.dot(pooled_attended, weight_wide, precision=lax.Precision.HIGHEST)
    unit_docs = normalize(pooled)
    kept_mask = keep_flags == 1
    slot_major = keep_flags.reshape(OWNERS, DOCS_DEV).T.reshape(-1)
    before = jnp.cumsum(slot_major) - slot_major
    doc_rank = before.reshape(DOCS_DEV, OWNERS).T.reshape(-1).astype(jnp.int32)
    doc_rank = jnp.where(kept_mask, doc_rank, -1).astype(jnp.int32)
    doc_rows = doc_rank % OWNERS * KEPT_DEV + doc_rank // OWNERS
    doc_rows = jnp.where(kept_mask, doc_rows, KEPT).astype(jnp.int32)
    doc_vectors = jnp.zeros((KEPT, OUT_DIM), jnp.bfloat16).at[doc_rows].set(unit_docs, mode='drop')
    owners = owner_map[list_ids].astype(jnp.int32)
    usable = kept_mask[:, None] & (token_ids != 0)
    positions = jnp.arange(DOC_LEN, dtype=jnp.int32)
    sort_keys = (doc_rank[:, None] * DOC_LEN + positions[None, :]).astype(jnp.int32)
    token_total = DOCS * DOC_LEN
    flat_keys = jnp.where(usable, sort_keys, token_total).reshape(-1).astype(jnp.int32)
    ordering = jnp.argsort(flat_keys, stable=True)
    ordered_keys = flat_keys[ordering]
    ordered_owner = owners.reshape(-1)[ordering]
    ordered_use = usable.reshape(-1)[ordering]
    member = ((ordered_owner[:, None] == jnp.arange(OWNERS, dtype=jnp.int32)[None, :]) & ordered_use[:, None]).astype(jnp.int32)
    running = jnp.cumsum(member, axis=0).astype(jnp.int32)
    within = jnp.take_along_axis(running, ordered_owner[:, None], axis=1)[:, 0] - 1
    dest_rows = jnp.where(ordered_use, ordered_owner * OWN_CAP + within, OWNERS * OWN_CAP).astype(jnp.int32)
    flat_tokens = unit_tokens.reshape(token_total, OUT_DIM)[ordering]
    token_vectors = jnp.zeros((OWNERS * OWN_CAP, OUT_DIM), jnp.bfloat16).at[dest_rows].set(flat_tokens, mode='drop')
    token_keys = jnp.full((OWNERS * OWN_CAP,), -1, jnp.int32).at[dest_rows].set(ordered_keys, mode='drop')
    return (doc_vectors, token_vectors, token_keys)
```

```python
import math

import jax
import jax.numpy as jnp
from jax import lax
from jax.sharding import PartitionSpec as P

HEAD_DIM = 128
F32 = jnp.float32
BF16 = jnp.bfloat16


def normalize(values):
    return (values * lax.rsqrt(jnp.mean(values * values, axis=-1, keepdims=True) + 1e-06)).astype(BF16)


def attend(query_states, key_states, value_states, token_ids):
    doc_count, length, features = query_states.shape
    kv_features = key_states.shape[2]
    kv_count = kv_features // HEAD_DIM
    group_size = features // kv_features
    queries = query_states.reshape(doc_count, length, kv_count, group_size, HEAD_DIM)
    keys_split = key_states.reshape(doc_count, length, kv_count, HEAD_DIM)
    values_split = value_states.reshape(doc_count, length, kv_count, HEAD_DIM)
    scores = jnp.einsum(
        "nqhgd,nshd->nhgqs", queries, keys_split, preferred_element_type=F32
    ) / math.sqrt(HEAD_DIM)
    present = token_ids != 0
    scores = jnp.where(present[:, None, None, None, :], scores, -jnp.inf)
    row_max = jnp.max(scores, axis=-1, keepdims=True)
    weights = jnp.exp(scores - row_max)
    weights = (weights / jnp.sum(weights, axis=-1, keepdims=True)).astype(BF16)
    attended = jnp.einsum("nhgqs,nshd->nqhgd", weights, values_split, preferred_element_type=F32)
    attended = attended.reshape(doc_count, length, features).astype(BF16)
    counts = jnp.sum(present.astype(F32), axis=1)
    pooled = (
        jnp.einsum("nt,ntf->nf", present.astype(BF16), attended, preferred_element_type=F32)
        / counts[:, None]
    )
    return attended, pooled


def exclusive_rows(mask):
    size = mask.shape[-1]
    at = jnp.arange(size, dtype=jnp.int32)
    upper = (at[:, None] < at[None, :]).astype(BF16)
    return jnp.dot(mask.astype(BF16), upper, preferred_element_type=F32).astype(jnp.int32)


def routing(codes, flags, me):
    n, docs, length = codes.shape
    place = jnp.arange(docs, dtype=jnp.int32)[None, :] * n + jnp.arange(n, dtype=jnp.int32)[:, None]
    place = place.reshape(-1)
    kept = flags.reshape(-1) == 1
    before = (place[None, :] < place[:, None]) & kept[None, :]
    rank = jnp.where(kept, jnp.sum(before.astype(jnp.int32), axis=1), -1)
    mine = (codes == me).reshape(n * docs, length)
    inner = exclusive_rows(mine)
    count = jnp.sum(mine.astype(jnp.int32), axis=1)
    earlier_rank = jnp.sum(jnp.where(before, count[None, :], 0), axis=1)
    position = earlier_rank[:, None] + inner
    by_source = count.reshape(n, docs)
    doc = jnp.arange(docs, dtype=jnp.int32)
    earlier_doc = jnp.sum(
        jnp.where(doc[None, None, :] < doc[None, :, None], by_source[:, None, :], 0), axis=2
    )
    slot = earlier_doc.reshape(-1)[:, None] + inner
    keys = rank[:, None] * length + jnp.arange(length, dtype=jnp.int32)[None, :]
    return rank, mine, position, slot, keys


def shards(
    query_states, key_states, value_states, out_weight, token_ids, keep_flags, list_ids, owner_map
):
    n = lax.axis_size("dp")
    me = lax.axis_index("dp").astype(jnp.int32)
    docs, length, features = query_states.shape
    rows = docs * length
    cap = 3 * rows // (2 * n)
    weight = lax.all_gather(out_weight, "dp", axis=0, tiled=True)

    lists = owner_map.shape[0]
    hit = list_ids.reshape(-1)[:, None] == jnp.arange(lists, dtype=jnp.int32)[None, :]
    owners = jnp.sum(jnp.where(hit, owner_map[None, :], 0), axis=1).reshape(docs, length)
    codes = jnp.where((keep_flags == 1)[:, None] & (token_ids != 0), owners, -1)
    info = jnp.concatenate([codes, jnp.broadcast_to(keep_flags[:, None], (docs, length))], axis=0)
    every = lax.all_gather(info, "dp")
    rank, mine, position, slot, keys = routing(every[:, :docs], every[:, docs:, 0], me)

    flat = codes.reshape(-1)
    member = (flat[None, :] == jnp.arange(n, dtype=jnp.int32)[:, None])
    at = jnp.arange(rows, dtype=jnp.int32)
    tri = (at[:, None] < at[None, :]).astype(BF16)
    within = jnp.dot(member.astype(BF16), tri, preferred_element_type=F32).astype(jnp.int32)
    pick = (
        member[:, None, :]
        & (within[:, None, :] == jnp.arange(cap, dtype=jnp.int32)[None, :, None])
    ).astype(BF16).reshape(n * cap, rows)

    attended, pooled = attend(query_states, key_states, value_states, token_ids)
    packed = jnp.dot(pick, attended.reshape(rows, features), preferred_element_type=F32).astype(BF16)
    arrived = lax.all_to_all(
        packed.reshape(n, cap, features), "dp", split_axis=0, concat_axis=0, tiled=True
    ).reshape(n * cap, features)
    high = pooled.astype(BF16)
    low = (pooled - high.astype(F32)).astype(BF16)
    every_doc = lax.all_gather(jnp.concatenate([high, low], axis=0), "dp")
    every_doc = jnp.concatenate([every_doc[:, :docs], every_doc[:, docs:]], axis=2).reshape(
        n * docs, 2 * features
    )

    mine_s = mine.reshape(n, rows)
    slot_s = jnp.where(mine_s, slot.reshape(n, rows), -1)
    fits = slot_s[:, None, :] == jnp.arange(cap, dtype=jnp.int32)[None, :, None]
    slot_position = jnp.sum(
        jnp.where(fits, position.reshape(n, 1, rows) + 1, 0), axis=2
    ).reshape(-1) - 1
    slot_key = jnp.sum(jnp.where(fits, keys.reshape(n, 1, rows) + 1, 0), axis=2).reshape(-1)
    order = jnp.arange(rows, dtype=jnp.int32)[:, None] == slot_position[None, :]
    token_keys = jnp.sum(jnp.where(order, slot_key[None, :], 0), axis=1) - 1
    sorted_rows = jnp.dot(order.astype(BF16), arrived, preferred_element_type=F32).astype(BF16)
    token_vectors = normalize(jnp.dot(sorted_rows, weight, preferred_element_type=F32))

    kept_slots = 3 * docs // 4
    wanted = jnp.arange(kept_slots, dtype=jnp.int32) * n + me
    picker = (rank[None, :] == wanted[:, None]).astype(BF16)
    chosen = jnp.dot(picker, every_doc, preferred_element_type=F32).astype(BF16)
    parts = jnp.concatenate([chosen[:, :features], chosen[:, features:]], axis=0)
    doc_sum = jnp.dot(parts, weight, preferred_element_type=F32)
    doc_vectors = normalize(doc_sum[:kept_slots] + doc_sum[kept_slots:])
    return (doc_vectors, token_vectors, token_keys)


def solution(mesh):
    return jax.shard_map(
        shards,
        mesh=mesh,
        in_specs=(
            P(("groups", "dp"), None, None),
            P(("groups", "dp"), None, None),
            P(("groups", "dp"), None, None),
            P("dp", None),
            P(("groups", "dp"), None),
            P(("groups", "dp")),
            P(("groups", "dp"), None),
            P("groups"),
        ),
        out_specs=(P(("groups", "dp"), None), P(("groups", "dp"), None), P(("groups", "dp"))),
        check_vma=False,
    )
```

```python
import functools
import math

import jax
import jax.numpy as jnp
from jax import lax
from jax.experimental import pallas as pl
from jax.experimental.pallas import tpu as pltpu
from jax.sharding import PartitionSpec as P

HEAD_DIM = 128
F32 = jnp.float32
BF16 = jnp.bfloat16


def normalize(values):
    return (values * lax.rsqrt(jnp.mean(values * values, axis=-1, keepdims=True) + 1e-06)).astype(BF16)


def attend(query_states, key_states, value_states, token_ids):
    doc_count, length, features = query_states.shape
    kv_features = key_states.shape[2]
    kv_count = kv_features // HEAD_DIM
    group_size = features // kv_features
    queries = query_states.reshape(doc_count, length, kv_count, group_size, HEAD_DIM)
    keys_split = key_states.reshape(doc_count, length, kv_count, HEAD_DIM)
    values_split = value_states.reshape(doc_count, length, kv_count, HEAD_DIM)
    scores = jnp.einsum(
        "nqhgd,nshd->nhgqs", queries, keys_split, preferred_element_type=F32
    ) / math.sqrt(HEAD_DIM)
    present = token_ids != 0
    scores = jnp.where(present[:, None, None, None, :], scores, -jnp.inf)
    row_max = jnp.max(scores, axis=-1, keepdims=True)
    weights = jnp.exp(scores - row_max)
    weights = (weights / jnp.sum(weights, axis=-1, keepdims=True)).astype(BF16)
    attended = jnp.einsum("nhgqs,nshd->nqhgd", weights, values_split, preferred_element_type=F32)
    attended = attended.reshape(doc_count, length, features).astype(BF16)
    counts = jnp.sum(present.astype(F32), axis=1)
    pooled = (
        jnp.einsum("nt,ntf->nf", present.astype(BF16), attended, preferred_element_type=F32)
        / counts[:, None]
    )
    return attended, pooled


def exclusive_rows(mask):
    size = mask.shape[-1]
    at = jnp.arange(size, dtype=jnp.int32)
    upper = (at[:, None] < at[None, :]).astype(BF16)
    return jnp.dot(mask.astype(BF16), upper, preferred_element_type=F32).astype(jnp.int32)


def routing(codes, flags, me):
    n, docs, length = codes.shape
    place = jnp.arange(docs, dtype=jnp.int32)[None, :] * n + jnp.arange(n, dtype=jnp.int32)[:, None]
    place = place.reshape(-1)
    kept = flags.reshape(-1) == 1
    before = (place[None, :] < place[:, None]) & kept[None, :]
    rank = jnp.where(kept, jnp.sum(before.astype(jnp.int32), axis=1), -1)
    mine = (codes == me).reshape(n * docs, length)
    inner = exclusive_rows(mine)
    count = jnp.sum(mine.astype(jnp.int32), axis=1)
    earlier_rank = jnp.sum(jnp.where(before, count[None, :], 0), axis=1)
    position = earlier_rank[:, None] + inner
    by_source = count.reshape(n, docs)
    doc = jnp.arange(docs, dtype=jnp.int32)
    earlier_doc = jnp.sum(
        jnp.where(doc[None, None, :] < doc[None, :, None], by_source[:, None, :], 0), axis=2
    )
    slot = earlier_doc.reshape(-1)[:, None] + inner
    keys = rank[:, None] * length + jnp.arange(length, dtype=jnp.int32)[None, :]
    return rank, mine, position, slot, keys


def exchange_kernel(
    n, w_ref, rows_ref, docs_ref, info_ref, w_all, rows_all, docs_all, info_all,
    w_send, w_recv, peer_send, peer_recv, own_sem,
):
    me = lax.axis_index("dp")
    planes = n // 4
    plane, spot = lax.div(me, 4), lax.rem(me, 4)
    core, column = lax.rem(spot, 2), lax.div(spot, 2)
    depth = w_ref.shape[0]
    mate = me + 1 - 2 * core
    beside = me + 2 - 4 * column

    barrier = pltpu.get_barrier_semaphore()

    def greet(k, _):
        pl.semaphore_signal(barrier, inc=1, device_id={"dp": lax.rem(me + k, n)}, device_id_type=pl.DeviceIdType.MESH)
        return 0

    lax.fori_loop(1, n, greet, 0)
    pl.semaphore_wait(barrier, n - 1)

    def span(block):
        return pl.ds(pl.multiple_of(block * depth, depth), depth)

    def block_copy(block, lane, target, source=None):
        return pltpu.make_async_remote_copy(
            src_ref=w_all.at[span(block)] if source is None else source,
            dst_ref=w_all.at[span(block)],
            send_sem=w_send.at[lane, block],
            recv_sem=w_recv.at[block],
            device_id={"dp": target},
            device_id_type=pl.DeviceIdType.MESH,
        )

    has_up, has_down = plane < planes - 1, plane > 0

    @pl.when(has_up)
    def _():
        block_copy(me, 0, me + 4, w_ref).start()

    @pl.when(has_down)
    def _():
        block_copy(me, 1, me - 4, w_ref).start()

    block_copy(me, 2, beside, w_ref).start()
    block_copy(me, 3, mate, w_ref).start()

    arrays = ((rows_ref, rows_all), (docs_ref, docs_all), (info_ref, info_all))
    owns = [pltpu.make_async_copy(w_ref, w_all.at[span(me)], own_sem.at[0])]
    owns.append(pltpu.make_async_copy(rows_ref.at[me], rows_all.at[me], own_sem.at[1]))
    owns.append(pltpu.make_async_copy(docs_ref, docs_all.at[me], own_sem.at[2]))
    owns.append(pltpu.make_async_copy(info_ref, info_all.at[me], own_sem.at[3]))
    for copy in owns:
        copy.start()

    def peer_copy(which, k, peer, slot):
        here, there = arrays[which]
        return pltpu.make_async_remote_copy(
            src_ref=here.at[peer] if which == 0 else here,
            dst_ref=there.at[slot],
            send_sem=peer_send.at[which, k],
            recv_sem=peer_recv.at[which, slot],
            device_id={"dp": peer},
            device_id_type=pl.DeviceIdType.MESH,
        )

    def push(k, _):
        for which in (2, 1, 0):
            peer_copy(which, k, lax.rem(me + k, n), me).start()
        return 0

    lax.fori_loop(1, n, push, 0)

    def side_block(block):
        return block + 2 - 4 * column

    def from_side(block):
        block_copy(side_block(block), 3, mate).wait_recv()
        block_copy(side_block(block), 3, mate).start()

    from_side(me)

    def hop(step, _):
        low, high = me - 4 * step, me + 4 * step

        @pl.when(plane - step >= 0)
        def _():
            block_copy(low, 2, beside).wait_recv()

            @pl.when(has_up)
            def _():
                block_copy(low, 0, me + 4).start()

            block_copy(low, 2, beside).start()
            block_copy(low, 3, mate).start()

        @pl.when(plane + step < planes)
        def _():
            block_copy(high, 2, beside).wait_recv()

            @pl.when(has_down)
            def _():
                block_copy(high, 1, me - 4).start()

            block_copy(high, 2, beside).start()
            block_copy(high, 3, mate).start()

        @pl.when(plane - step >= 0)
        def _():
            from_side(low)

        @pl.when(plane + step < planes)
        def _():
            from_side(high)

        return 0

    lax.fori_loop(1, planes, hop, 0)

    def finish(at, _):
        line = at * 4 + spot
        block_copy(line, 2, beside).wait_send()
        block_copy(line, 3, mate).wait_send()
        block_copy(side_block(line), 3, mate).wait_send()
        other = at * 4 + 1 - core
        block_copy(other, 3, mate).wait_recv()
        block_copy(other + 2, 3, mate).wait_recv()

        @pl.when(has_up & (at <= plane))
        def _():
            block_copy(line, 0, me + 4).wait_send()

        @pl.when(has_down & (at >= plane))
        def _():
            block_copy(line, 1, me - 4).wait_send()

        return 0

    lax.fori_loop(0, planes, finish, 0)

    def settle(k, _):
        for which in range(3):
            peer_copy(which, k, lax.rem(me + k, n), me).wait_send()
            peer_copy(which, k, lax.rem(me + k, n), lax.rem(me + n - k, n)).wait_recv()
        return 0

    lax.fori_loop(1, n, settle, 0)
    for copy in owns:
        copy.wait()


def exchange(n, weight, rows, docs, info):
    anywhere = pl.BlockSpec(memory_space=pl.ANY)
    shape = jax.ShapeDtypeStruct
    return pl.pallas_call(
        functools.partial(exchange_kernel, n),
        out_shape=(
            shape((n * weight.shape[0], weight.shape[1]), weight.dtype),
            shape(rows.shape, rows.dtype),
            shape((n,) + docs.shape, docs.dtype),
            shape((n,) + info.shape, info.dtype),
        ),
        in_specs=[anywhere] * 4,
        out_specs=(anywhere,) * 4,
        scratch_shapes=[
            pltpu.SemaphoreType.DMA((4, n)),
            pltpu.SemaphoreType.DMA((n,)),
            pltpu.SemaphoreType.DMA((3, n)),
            pltpu.SemaphoreType.DMA((3, n)),
            pltpu.SemaphoreType.DMA((4,)),
        ],
        compiler_params=pltpu.CompilerParams(collective_id=0, has_side_effects=True),
    )(weight, rows, docs, info)


def shards(
    query_states, key_states, value_states, out_weight, token_ids, keep_flags, list_ids, owner_map
):
    n = lax.axis_size("dp")
    me = lax.axis_index("dp").astype(jnp.int32)
    docs, length, features = query_states.shape
    rows = docs * length
    cap = -(-3 * rows // (2 * n) // 16) * 16

    lists = owner_map.shape[0]
    hit = list_ids.reshape(-1)[:, None] == jnp.arange(lists, dtype=jnp.int32)[None, :]
    owners = jnp.sum(jnp.where(hit, owner_map[None, :], 0), axis=1).reshape(docs, length)
    codes = jnp.where((keep_flags == 1)[:, None] & (token_ids != 0), owners, -1)
    info = jnp.concatenate([codes, jnp.broadcast_to(keep_flags[:, None], (docs, length))], axis=0)
    flat = codes.reshape(-1)
    member = (flat[None, :] == jnp.arange(n, dtype=jnp.int32)[:, None])
    at = jnp.arange(rows, dtype=jnp.int32)
    tri = (at[:, None] < at[None, :]).astype(BF16)
    within = jnp.dot(member.astype(BF16), tri, preferred_element_type=F32).astype(jnp.int32)
    pick = (
        member[:, None, :]
        & (within[:, None, :] == jnp.arange(cap, dtype=jnp.int32)[None, :, None])
    ).astype(BF16).reshape(n * cap, rows)

    attended, pooled = attend(query_states, key_states, value_states, token_ids)
    packed = jnp.dot(pick, attended.reshape(rows, features), preferred_element_type=F32).astype(BF16)
    sent_docs = pooled.astype(BF16).reshape(16, docs * features // 16)
    weight, arrived, every_doc, every = exchange(
        n, out_weight, packed.reshape(n, cap, features), sent_docs, info
    )
    arrived = arrived.reshape(n * cap, features)
    every_doc = every_doc.reshape(n * docs, features)
    rank, mine, position, slot, keys = routing(every[:, :docs], every[:, docs:, 0], me)

    mine_s = mine.reshape(n, rows)
    slot_s = jnp.where(mine_s, slot.reshape(n, rows), -1)
    fits = slot_s[:, None, :] == jnp.arange(cap, dtype=jnp.int32)[None, :, None]
    slot_position = jnp.sum(
        jnp.where(fits, position.reshape(n, 1, rows) + 1, 0), axis=2
    ).reshape(-1) - 1
    slot_key = jnp.sum(jnp.where(fits, keys.reshape(n, 1, rows) + 1, 0), axis=2).reshape(-1)
    order = jnp.arange(rows, dtype=jnp.int32)[:, None] == slot_position[None, :]
    token_keys = jnp.sum(jnp.where(order, slot_key[None, :], 0), axis=1) - 1
    sorted_rows = jnp.dot(order.astype(BF16), arrived, preferred_element_type=F32).astype(BF16)
    token_vectors = normalize(jnp.dot(sorted_rows, weight, preferred_element_type=F32))

    kept_slots = 3 * docs // 4
    wanted = jnp.arange(kept_slots, dtype=jnp.int32) * n + me
    picker = (rank[None, :] == wanted[:, None]).astype(BF16)
    chosen = jnp.dot(picker, every_doc, preferred_element_type=F32).astype(BF16)
    doc_vectors = normalize(jnp.dot(chosen, weight, preferred_element_type=F32))
    return (doc_vectors, token_vectors, token_keys)


def solution(mesh):
    return jax.shard_map(
        shards,
        mesh=mesh,
        in_specs=(
            P(("groups", "dp"), None, None),
            P(("groups", "dp"), None, None),
            P(("groups", "dp"), None, None),
            P("dp", None),
            P(("groups", "dp"), None),
            P(("groups", "dp")),
            P(("groups", "dp"), None),
            P("groups"),
        ),
        out_specs=(P(("groups", "dp"), None), P(("groups", "dp"), None), P(("groups", "dp"))),
        check_vma=False,
    )
```

```python
import functools
import math

import jax
import jax.numpy as jnp
from jax import lax
from jax.experimental import pallas as pl
from jax.experimental.pallas import tpu as pltpu
from jax.sharding import PartitionSpec as P

HEAD_DIM = 128
F32 = jnp.float32
BF16 = jnp.bfloat16


def normalize(values):
    return (values * lax.rsqrt(jnp.mean(values * values, axis=-1, keepdims=True) + 1e-06)).astype(BF16)


def attend(query_states, key_states, value_states, token_ids):
    doc_count, length, features = query_states.shape
    kv_features = key_states.shape[2]
    kv_count = kv_features // HEAD_DIM
    group_size = features // kv_features
    queries = query_states.reshape(doc_count, length, kv_count, group_size, HEAD_DIM)
    keys_split = key_states.reshape(doc_count, length, kv_count, HEAD_DIM)
    values_split = value_states.reshape(doc_count, length, kv_count, HEAD_DIM)
    scores = jnp.einsum(
        "nqhgd,nshd->nhgqs", queries, keys_split, preferred_element_type=F32
    ) / math.sqrt(HEAD_DIM)
    present = token_ids != 0
    scores = jnp.where(present[:, None, None, None, :], scores, -jnp.inf)
    row_max = jnp.max(scores, axis=-1, keepdims=True)
    weights = jnp.exp(scores - row_max)
    weights = (weights / jnp.sum(weights, axis=-1, keepdims=True)).astype(BF16)
    attended = jnp.einsum("nhgqs,nshd->nqhgd", weights, values_split, preferred_element_type=F32)
    attended = attended.reshape(doc_count, length, features).astype(BF16)
    counts = jnp.sum(present.astype(F32), axis=1)
    pooled = (
        jnp.einsum("nt,ntf->nf", present.astype(BF16), attended, preferred_element_type=F32)
        / counts[:, None]
    )
    return attended, pooled


def exclusive_rows(mask):
    size = mask.shape[-1]
    at = jnp.arange(size, dtype=jnp.int32)
    upper = (at[:, None] < at[None, :]).astype(BF16)
    return jnp.dot(mask.astype(BF16), upper, preferred_element_type=F32).astype(jnp.int32)


def routing(codes, flags, me):
    n, docs, length = codes.shape
    place = jnp.arange(docs, dtype=jnp.int32)[None, :] * n + jnp.arange(n, dtype=jnp.int32)[:, None]
    place = place.reshape(-1)
    kept = flags.reshape(-1) == 1
    before = (place[None, :] < place[:, None]) & kept[None, :]
    rank = jnp.where(kept, jnp.sum(before.astype(jnp.int32), axis=1), -1)
    mine = (codes == me).reshape(n * docs, length)
    inner = exclusive_rows(mine)
    count = jnp.sum(mine.astype(jnp.int32), axis=1)
    earlier_rank = jnp.sum(jnp.where(before, count[None, :], 0), axis=1)
    position = earlier_rank[:, None] + inner
    by_source = count.reshape(n, docs)
    doc = jnp.arange(docs, dtype=jnp.int32)
    earlier_doc = jnp.sum(
        jnp.where(doc[None, None, :] < doc[None, :, None], by_source[:, None, :], 0), axis=2
    )
    slot = earlier_doc.reshape(-1)[:, None] + inner
    keys = rank[:, None] * length + jnp.arange(length, dtype=jnp.int32)[None, :]
    return rank, mine, position, slot, keys


def exchange_kernel(
    n, w_ref, rows_ref, docs_ref, info_ref, w_all, rows_all, docs_all, info_all,
    w_send, w_recv, peer_send, peer_recv, own_sem,
):
    me = lax.axis_index("dp")
    planes = n // 4
    plane, spot = lax.div(me, 4), lax.rem(me, 4)
    core, column = lax.rem(spot, 2), lax.div(spot, 2)
    depth = w_ref.shape[0]
    mate = me + 1 - 2 * core
    beside = me + 2 - 4 * column

    barrier = pltpu.get_barrier_semaphore()

    def greet(k, _):
        pl.semaphore_signal(barrier, inc=1, device_id={"dp": lax.rem(me + k, n)}, device_id_type=pl.DeviceIdType.MESH)
        return 0

    lax.fori_loop(1, n, greet, 0)
    pl.semaphore_wait(barrier, n - 1)

    def span(block):
        return pl.ds(pl.multiple_of(block * depth, depth), depth)

    def block_copy(block, lane, target, source=None):
        return pltpu.make_async_remote_copy(
            src_ref=w_all.at[span(block)] if source is None else source,
            dst_ref=w_all.at[span(block)],
            send_sem=w_send.at[lane, block],
            recv_sem=w_recv.at[block],
            device_id={"dp": target},
            device_id_type=pl.DeviceIdType.MESH,
        )

    has_up, has_down = plane < planes - 1, plane > 0

    @pl.when(has_up)
    def _():
        block_copy(me, 0, me + 4, w_ref).start()

    @pl.when(has_down)
    def _():
        block_copy(me, 1, me - 4, w_ref).start()

    block_copy(me, 2, beside, w_ref).start()
    block_copy(me, 3, mate, w_ref).start()

    arrays = ((rows_ref, rows_all), (docs_ref, docs_all), (info_ref, info_all))
    owns = [pltpu.make_async_copy(w_ref, w_all.at[span(me)], own_sem.at[0])]
    owns.append(pltpu.make_async_copy(rows_ref.at[me], rows_all.at[me], own_sem.at[1]))
    owns.append(pltpu.make_async_copy(docs_ref, docs_all.at[me], own_sem.at[2]))
    owns.append(pltpu.make_async_copy(info_ref, info_all.at[me], own_sem.at[3]))
    for copy in owns:
        copy.start()

    def peer_copy(which, k, peer, slot):
        here, there = arrays[which]
        return pltpu.make_async_remote_copy(
            src_ref=here.at[peer] if which == 0 else here,
            dst_ref=there.at[slot],
            send_sem=peer_send.at[which, k],
            recv_sem=peer_recv.at[which, slot],
            device_id={"dp": peer},
            device_id_type=pl.DeviceIdType.MESH,
        )

    def target(k):
        ahead = lax.rem(plane + lax.div(k, 4), planes)
        return ahead * 4 + lax.rem(spot + lax.rem(k, 4), 4)

    def origin(k):
        behind = lax.rem(plane + planes - lax.div(k, 4), planes)
        return behind * 4 + lax.rem(spot + 4 - lax.rem(k, 4), 4)

    def push_small(k, _):
        for which in (2, 1):
            peer_copy(which, k, target(k), me).start()
        return 0

    def push_rows(k, _):
        peer_copy(0, k, target(k), me).start()
        return 0

    lax.fori_loop(1, n, push_small, 0)
    lax.fori_loop(1, 4, push_rows, 0)

    def side_block(block):
        return block + 2 - 4 * column

    def from_side(block):
        block_copy(side_block(block), 3, mate).wait_recv()
        block_copy(side_block(block), 3, mate).start()

    from_side(me)

    def hop(step, _):
        low, high = me - 4 * step, me + 4 * step

        @pl.when(plane - step >= 0)
        def _():
            block_copy(low, 2, beside).wait_recv()

            @pl.when(has_up)
            def _():
                block_copy(low, 0, me + 4).start()

            block_copy(low, 2, beside).start()
            block_copy(low, 3, mate).start()

        @pl.when(plane + step < planes)
        def _():
            block_copy(high, 2, beside).wait_recv()

            @pl.when(has_down)
            def _():
                block_copy(high, 1, me - 4).start()

            block_copy(high, 2, beside).start()
            block_copy(high, 3, mate).start()

        lax.fori_loop(4 * step, 4 * step + 4, push_rows, 0)

        @pl.when(plane - step >= 0)
        def _():
            from_side(low)

        @pl.when(plane + step < planes)
        def _():
            from_side(high)

        return 0

    lax.fori_loop(1, planes, hop, 0)

    def finish(at, _):
        line = at * 4 + spot
        block_copy(line, 2, beside).wait_send()
        block_copy(line, 3, mate).wait_send()
        block_copy(side_block(line), 3, mate).wait_send()
        other = at * 4 + 1 - core
        block_copy(other, 3, mate).wait_recv()
        block_copy(other + 2, 3, mate).wait_recv()

        @pl.when(has_up & (at <= plane))
        def _():
            block_copy(line, 0, me + 4).wait_send()

        @pl.when(has_down & (at >= plane))
        def _():
            block_copy(line, 1, me - 4).wait_send()

        return 0

    lax.fori_loop(0, planes, finish, 0)

    def settle(k, _):
        for which in range(3):
            peer_copy(which, k, target(k), me).wait_send()
            peer_copy(which, k, target(k), origin(k)).wait_recv()
        return 0

    lax.fori_loop(1, n, settle, 0)
    for copy in owns:
        copy.wait()


def exchange(n, weight, rows, docs, info):
    anywhere = pl.BlockSpec(memory_space=pl.ANY)
    shape = jax.ShapeDtypeStruct
    return pl.pallas_call(
        functools.partial(exchange_kernel, n),
        out_shape=(
            shape((n * weight.shape[0], weight.shape[1]), weight.dtype),
            shape(rows.shape, rows.dtype),
            shape((n,) + docs.shape, docs.dtype),
            shape((n,) + info.shape, info.dtype),
        ),
        in_specs=[anywhere] * 4,
        out_specs=(anywhere,) * 4,
        scratch_shapes=[
            pltpu.SemaphoreType.DMA((4, n)),
            pltpu.SemaphoreType.DMA((n,)),
            pltpu.SemaphoreType.DMA((3, n)),
            pltpu.SemaphoreType.DMA((3, n)),
            pltpu.SemaphoreType.DMA((4,)),
        ],
        compiler_params=pltpu.CompilerParams(collective_id=0, has_side_effects=True),
    )(weight, rows, docs, info)


def shards(
    query_states, key_states, value_states, out_weight, token_ids, keep_flags, list_ids, owner_map
):
    n = lax.axis_size("dp")
    me = lax.axis_index("dp").astype(jnp.int32)
    docs, length, features = query_states.shape
    rows = docs * length
    cap = -(-3 * rows // (2 * n) // 16) * 16

    lists = owner_map.shape[0]
    hit = list_ids.reshape(-1)[:, None] == jnp.arange(lists, dtype=jnp.int32)[None, :]
    owners = jnp.sum(jnp.where(hit, owner_map[None, :], 0), axis=1).reshape(docs, length)
    codes = jnp.where((keep_flags == 1)[:, None] & (token_ids != 0), owners, -1)
    info = jnp.concatenate([codes, jnp.broadcast_to(keep_flags[:, None], (docs, length))], axis=0)
    flat = codes.reshape(-1)
    member = (flat[None, :] == jnp.arange(n, dtype=jnp.int32)[:, None])
    at = jnp.arange(rows, dtype=jnp.int32)
    tri = (at[:, None] < at[None, :]).astype(BF16)
    within = jnp.dot(member.astype(BF16), tri, preferred_element_type=F32).astype(jnp.int32)
    pick = (
        member[:, None, :]
        & (within[:, None, :] == jnp.arange(cap, dtype=jnp.int32)[None, :, None])
    ).astype(BF16).reshape(n * cap, rows)

    attended, pooled = attend(query_states, key_states, value_states, token_ids)
    packed = jnp.dot(pick, attended.reshape(rows, features), preferred_element_type=F32).astype(BF16)
    sent_docs = pooled.astype(BF16).reshape(16, docs * features // 16)
    weight, arrived, every_doc, every = exchange(
        n, out_weight, packed.reshape(n, cap, features), sent_docs, info
    )
    arrived = arrived.reshape(n * cap, features)
    every_doc = every_doc.reshape(n * docs, features)
    rank, mine, position, slot, keys = routing(every[:, :docs], every[:, docs:, 0], me)

    mine_s = mine.reshape(n, rows)
    slot_s = jnp.where(mine_s, slot.reshape(n, rows), -1)
    fits = slot_s[:, None, :] == jnp.arange(cap, dtype=jnp.int32)[None, :, None]
    slot_position = jnp.sum(
        jnp.where(fits, position.reshape(n, 1, rows) + 1, 0), axis=2
    ).reshape(-1) - 1
    slot_key = jnp.sum(jnp.where(fits, keys.reshape(n, 1, rows) + 1, 0), axis=2).reshape(-1)
    order = jnp.arange(rows, dtype=jnp.int32)[:, None] == slot_position[None, :]
    token_keys = jnp.sum(jnp.where(order, slot_key[None, :], 0), axis=1) - 1
    sorted_rows = jnp.dot(order.astype(BF16), arrived, preferred_element_type=F32).astype(BF16)
    token_vectors = normalize(jnp.dot(sorted_rows, weight, preferred_element_type=F32))

    kept_slots = 3 * docs // 4
    wanted = jnp.arange(kept_slots, dtype=jnp.int32) * n + me
    picker = (rank[None, :] == wanted[:, None]).astype(BF16)
    chosen = jnp.dot(picker, every_doc, preferred_element_type=F32).astype(BF16)
    doc_vectors = normalize(jnp.dot(chosen, weight, preferred_element_type=F32))
    return (doc_vectors, token_vectors, token_keys)


def solution(mesh):
    return jax.shard_map(
        shards,
        mesh=mesh,
        in_specs=(
            P(("groups", "dp"), None, None),
            P(("groups", "dp"), None, None),
            P(("groups", "dp"), None, None),
            P("dp", None),
            P(("groups", "dp"), None),
            P(("groups", "dp")),
            P(("groups", "dp"), None),
            P("groups"),
        ),
        out_specs=(P(("groups", "dp"), None), P(("groups", "dp"), None), P(("groups", "dp"))),
        check_vma=False,
    )
```

```python
import functools
import math

import jax
import jax.numpy as jnp
from jax import lax
from jax.experimental import pallas as pl
from jax.experimental.pallas import tpu as pltpu
from jax.sharding import PartitionSpec as P

HEAD_DIM = 128
F32 = jnp.float32
BF16 = jnp.bfloat16


def normalize(values):
    return (values * lax.rsqrt(jnp.mean(values * values, axis=-1, keepdims=True) + 1e-06)).astype(BF16)


def attend(query_states, key_states, value_states, token_ids):
    doc_count, length, features = query_states.shape
    kv_features = key_states.shape[2]
    kv_count = kv_features // HEAD_DIM
    group_size = features // kv_features
    queries = query_states.reshape(doc_count, length, kv_count, group_size, HEAD_DIM)
    keys_split = key_states.reshape(doc_count, length, kv_count, HEAD_DIM)
    values_split = value_states.reshape(doc_count, length, kv_count, HEAD_DIM)
    scores = jnp.einsum(
        "nqhgd,nshd->nhgqs", queries, keys_split, preferred_element_type=F32
    ) / math.sqrt(HEAD_DIM)
    present = token_ids != 0
    scores = jnp.where(present[:, None, None, None, :], scores, -jnp.inf)
    row_max = jnp.max(scores, axis=-1, keepdims=True)
    weights = jnp.exp(scores - row_max)
    weights = (weights / jnp.sum(weights, axis=-1, keepdims=True)).astype(BF16)
    attended = jnp.einsum("nhgqs,nshd->nqhgd", weights, values_split, preferred_element_type=F32)
    attended = attended.reshape(doc_count, length, features).astype(BF16)
    counts = jnp.sum(present.astype(F32), axis=1)
    pooled = (
        jnp.einsum("nt,ntf->nf", present.astype(BF16), attended, preferred_element_type=F32)
        / counts[:, None]
    )
    return attended, pooled


def exclusive_rows(mask):
    size = mask.shape[-1]
    at = jnp.arange(size, dtype=jnp.int32)
    upper = (at[:, None] < at[None, :]).astype(BF16)
    return jnp.dot(mask.astype(BF16), upper, preferred_element_type=F32).astype(jnp.int32)


def routing(codes, flags, me):
    n, docs, length = codes.shape
    place = jnp.arange(docs, dtype=jnp.int32)[None, :] * n + jnp.arange(n, dtype=jnp.int32)[:, None]
    place = place.reshape(-1)
    kept = flags.reshape(-1) == 1
    before = (place[None, :] < place[:, None]) & kept[None, :]
    rank = jnp.where(kept, jnp.sum(before.astype(jnp.int32), axis=1), -1)
    mine = (codes == me).reshape(n * docs, length)
    inner = exclusive_rows(mine)
    count = jnp.sum(mine.astype(jnp.int32), axis=1)
    earlier_rank = jnp.sum(jnp.where(before, count[None, :], 0), axis=1)
    position = earlier_rank[:, None] + inner
    by_source = count.reshape(n, docs)
    doc = jnp.arange(docs, dtype=jnp.int32)
    earlier_doc = jnp.sum(
        jnp.where(doc[None, None, :] < doc[None, :, None], by_source[:, None, :], 0), axis=2
    )
    slot = earlier_doc.reshape(-1)[:, None] + inner
    keys = rank[:, None] * length + jnp.arange(length, dtype=jnp.int32)[None, :]
    return rank, mine, position, slot, keys


def exchange_kernel(
    n, w_ref, rows_ref, docs_ref, info_ref, w_all, rows_all, docs_all, info_all,
    w_send, w_recv, peer_send, peer_recv, own_sem,
):
    me = lax.axis_index("dp")
    planes = n // 4
    plane, spot = lax.div(me, 4), lax.rem(me, 4)
    core, column = lax.rem(spot, 2), lax.div(spot, 2)
    depth = w_ref.shape[0]
    mate = me + 1 - 2 * core
    beside = me + 2 - 4 * column

    barrier = pltpu.get_barrier_semaphore()

    def greet(k, _):
        pl.semaphore_signal(barrier, inc=1, device_id={"dp": lax.rem(me + k, n)}, device_id_type=pl.DeviceIdType.MESH)
        return 0

    lax.fori_loop(1, n, greet, 0)
    pl.semaphore_wait(barrier, n - 1)

    def span(block):
        return pl.ds(pl.multiple_of(block * depth, depth), depth)

    def block_copy(block, lane, target, source=None):
        return pltpu.make_async_remote_copy(
            src_ref=w_all.at[span(block)] if source is None else source,
            dst_ref=w_all.at[span(block)],
            send_sem=w_send.at[lane, block],
            recv_sem=w_recv.at[block],
            device_id={"dp": target},
            device_id_type=pl.DeviceIdType.MESH,
        )

    has_up, has_down = plane < planes - 1, plane > 0

    @pl.when(has_up)
    def _():
        block_copy(me, 0, me + 4, w_ref).start()

    @pl.when(has_down)
    def _():
        block_copy(me, 1, me - 4, w_ref).start()

    block_copy(me, 2, beside, w_ref).start()
    block_copy(me, 3, mate, w_ref).start()

    arrays = ((rows_ref, rows_all), (docs_ref, docs_all), (info_ref, info_all))
    owns = [pltpu.make_async_copy(w_ref, w_all.at[span(me)], own_sem.at[0])]
    owns.append(pltpu.make_async_copy(rows_ref.at[me], rows_all.at[me], own_sem.at[1]))
    owns.append(pltpu.make_async_copy(docs_ref, docs_all.at[me], own_sem.at[2]))
    owns.append(pltpu.make_async_copy(info_ref, info_all.at[me], own_sem.at[3]))
    for copy in owns:
        copy.start()

    def peer_copy(which, k, peer, slot):
        here, there = arrays[which]
        return pltpu.make_async_remote_copy(
            src_ref=here.at[peer] if which == 0 else here,
            dst_ref=there.at[slot],
            send_sem=peer_send.at[which, k],
            recv_sem=peer_recv.at[which, slot],
            device_id={"dp": peer},
            device_id_type=pl.DeviceIdType.MESH,
        )

    def target(k):
        ahead = lax.rem(plane + lax.div(k, 4), planes)
        return ahead * 4 + lax.rem(spot + lax.rem(k, 4), 4)

    def origin(k):
        behind = lax.rem(plane + planes - lax.div(k, 4), planes)
        return behind * 4 + lax.rem(spot + 4 - lax.rem(k, 4), 4)

    def push_small(k, _):
        for which in (2, 1):
            peer_copy(which, k, target(k), me).start()
        return 0

    def push_rows(k, _):
        peer_copy(0, k, target(k), me).start()
        return 0

    lax.fori_loop(1, n, push_small, 0)
    lax.fori_loop(1, 4, push_rows, 0)

    def side_block(block):
        return block + 2 - 4 * column

    def from_side(block):
        block_copy(side_block(block), 3, mate).wait_recv()
        block_copy(side_block(block), 3, mate).start()

    from_side(me)

    def hop(step, _):
        low, high = me - 4 * step, me + 4 * step

        @pl.when(plane - step >= 0)
        def _():
            block_copy(low, 2, beside).wait_recv()

            @pl.when(has_up)
            def _():
                block_copy(low, 0, me + 4).start()

            block_copy(low, 2, beside).start()
            block_copy(low, 3, mate).start()

        @pl.when(plane + step < planes)
        def _():
            block_copy(high, 2, beside).wait_recv()

            @pl.when(has_down)
            def _():
                block_copy(high, 1, me - 4).start()

            block_copy(high, 2, beside).start()
            block_copy(high, 3, mate).start()

        lax.fori_loop(4 * step, 4 * step + 4, push_rows, 0)

        @pl.when(plane - step >= 0)
        def _():
            from_side(low)

        @pl.when(plane + step < planes)
        def _():
            from_side(high)

        return 0

    lax.fori_loop(1, planes, hop, 0)

    def finish(at, _):
        line = at * 4 + spot
        block_copy(line, 2, beside).wait_send()
        block_copy(line, 3, mate).wait_send()
        block_copy(side_block(line), 3, mate).wait_send()
        other = at * 4 + 1 - core
        block_copy(other, 3, mate).wait_recv()
        block_copy(other + 2, 3, mate).wait_recv()

        @pl.when(has_up & (at <= plane))
        def _():
            block_copy(line, 0, me + 4).wait_send()

        @pl.when(has_down & (at >= plane))
        def _():
            block_copy(line, 1, me - 4).wait_send()

        return 0

    lax.fori_loop(0, planes, finish, 0)

    def settle(k, _):
        for which in range(3):
            peer_copy(which, k, target(k), me).wait_send()
            peer_copy(which, k, target(k), origin(k)).wait_recv()
        return 0

    lax.fori_loop(1, n, settle, 0)
    for copy in owns:
        copy.wait()


def exchange(n, weight, rows, docs, info):
    anywhere = pl.BlockSpec(memory_space=pl.ANY)
    shape = jax.ShapeDtypeStruct
    return pl.pallas_call(
        functools.partial(exchange_kernel, n),
        out_shape=(
            shape((n * weight.shape[0], weight.shape[1]), weight.dtype),
            shape(rows.shape, rows.dtype),
            shape((n,) + docs.shape, docs.dtype),
            shape((n,) + info.shape, info.dtype),
        ),
        in_specs=[anywhere] * 4,
        out_specs=(anywhere,) * 4,
        scratch_shapes=[
            pltpu.SemaphoreType.DMA((4, n)),
            pltpu.SemaphoreType.DMA((n,)),
            pltpu.SemaphoreType.DMA((3, n)),
            pltpu.SemaphoreType.DMA((3, n)),
            pltpu.SemaphoreType.DMA((4,)),
        ],
        compiler_params=pltpu.CompilerParams(collective_id=0, has_side_effects=True),
    )(weight, rows, docs, info)


def place_kernel(position_ref, arrived_ref, w_ref, out_ref):
    tile = out_ref.shape[0]
    row = lax.broadcasted_iota(jnp.int32, (tile, position_ref.shape[1]), 0) + pl.program_id(0) * tile
    order = jnp.where(row == position_ref[...], 1.0, 0.0).astype(BF16)
    chosen = jnp.dot(order, arrived_ref[...], preferred_element_type=F32).astype(BF16)
    out_ref[...] = normalize(jnp.dot(chosen, w_ref[...], preferred_element_type=F32))


def place(rows, positions, arrived, weight):
    width = weight.shape[1]
    tile = min(rows, 256)
    whole = lambda array: pl.BlockSpec(array.shape, lambda i: (0, 0))
    return pl.pallas_call(
        place_kernel,
        grid=(rows // tile,),
        out_shape=jax.ShapeDtypeStruct((rows, width), BF16),
        in_specs=[whole(positions), whole(arrived), whole(weight)],
        out_specs=pl.BlockSpec((tile, width), lambda i: (i, 0)),
        compiler_params=pltpu.CompilerParams(vmem_limit_bytes=50 * 2**20),
    )(positions, arrived, weight)


def shards(
    query_states, key_states, value_states, out_weight, token_ids, keep_flags, list_ids, owner_map
):
    n = lax.axis_size("dp")
    me = lax.axis_index("dp").astype(jnp.int32)
    docs, length, features = query_states.shape
    rows = docs * length
    cap = -(-3 * rows // (2 * n) // 16) * 16

    lists = owner_map.shape[0]
    hit = list_ids.reshape(-1)[:, None] == jnp.arange(lists, dtype=jnp.int32)[None, :]
    owners = jnp.sum(jnp.where(hit, owner_map[None, :], 0), axis=1).reshape(docs, length)
    codes = jnp.where((keep_flags == 1)[:, None] & (token_ids != 0), owners, -1)
    info = jnp.concatenate([codes, jnp.broadcast_to(keep_flags[:, None], (docs, length))], axis=0)
    flat = codes.reshape(-1)
    member = (flat[None, :] == jnp.arange(n, dtype=jnp.int32)[:, None])
    at = jnp.arange(rows, dtype=jnp.int32)
    tri = (at[:, None] < at[None, :]).astype(BF16)
    within = jnp.dot(member.astype(BF16), tri, preferred_element_type=F32).astype(jnp.int32)
    pick = (
        member[:, None, :]
        & (within[:, None, :] == jnp.arange(cap, dtype=jnp.int32)[None, :, None])
    ).astype(BF16).reshape(n * cap, rows)

    attended, pooled = attend(query_states, key_states, value_states, token_ids)
    packed = jnp.dot(pick, attended.reshape(rows, features), preferred_element_type=F32).astype(BF16)
    sent_docs = pooled.astype(BF16).reshape(16, docs * features // 16)
    weight, arrived, every_doc, every = exchange(
        n, out_weight, packed.reshape(n, cap, features), sent_docs, info
    )
    arrived = arrived.reshape(n * cap, features)
    every_doc = every_doc.reshape(n * docs, features)
    rank, mine, position, slot, keys = routing(every[:, :docs], every[:, docs:, 0], me)

    mine_s = mine.reshape(n, rows)
    slot_s = jnp.where(mine_s, slot.reshape(n, rows), -1)
    fits = slot_s[:, None, :] == jnp.arange(cap, dtype=jnp.int32)[None, :, None]
    slot_position = jnp.sum(
        jnp.where(fits, position.reshape(n, 1, rows) + 1, 0), axis=2
    ).reshape(-1) - 1
    slot_key = jnp.sum(jnp.where(fits, keys.reshape(n, 1, rows) + 1, 0), axis=2).reshape(-1)
    order = jnp.arange(rows, dtype=jnp.int32)[:, None] == slot_position[None, :]
    token_keys = jnp.sum(jnp.where(order, slot_key[None, :], 0), axis=1) - 1
    token_vectors = place(rows, slot_position[None, :], arrived, weight)

    kept_slots = 3 * docs // 4
    wanted = jnp.arange(kept_slots, dtype=jnp.int32) * n + me
    picker = (rank[None, :] == wanted[:, None]).astype(BF16)
    chosen = jnp.dot(picker, every_doc, preferred_element_type=F32).astype(BF16)
    doc_vectors = normalize(jnp.dot(chosen, weight, preferred_element_type=F32))
    return (doc_vectors, token_vectors, token_keys)


def solution(mesh):
    return jax.shard_map(
        shards,
        mesh=mesh,
        in_specs=(
            P(("groups", "dp"), None, None),
            P(("groups", "dp"), None, None),
            P(("groups", "dp"), None, None),
            P("dp", None),
            P(("groups", "dp"), None),
            P(("groups", "dp")),
            P(("groups", "dp"), None),
            P("groups"),
        ),
        out_specs=(P(("groups", "dp"), None), P(("groups", "dp"), None), P(("groups", "dp"))),
        check_vma=False,
    )
```

```python
import functools
import math

import jax
import jax.numpy as jnp
from jax import lax
from jax.experimental import pallas as pl
from jax.experimental.pallas import tpu as pltpu
from jax.sharding import PartitionSpec as P

HEAD_DIM = 128
F32 = jnp.float32
BF16 = jnp.bfloat16


def normalize(values):
    return (values * lax.rsqrt(jnp.mean(values * values, axis=-1, keepdims=True) + 1e-06)).astype(BF16)


def attend(query_states, key_states, value_states, token_ids):
    doc_count, length, features = query_states.shape
    kv_features = key_states.shape[2]
    kv_count = kv_features // HEAD_DIM
    group_size = features // kv_features
    queries = query_states.reshape(doc_count, length, kv_count, group_size, HEAD_DIM)
    keys_split = key_states.reshape(doc_count, length, kv_count, HEAD_DIM)
    values_split = value_states.reshape(doc_count, length, kv_count, HEAD_DIM)
    scores = jnp.einsum(
        "nqhgd,nshd->nhgqs", queries, keys_split, preferred_element_type=F32
    ) / math.sqrt(HEAD_DIM)
    present = token_ids != 0
    scores = jnp.where(present[:, None, None, None, :], scores, -jnp.inf)
    row_max = jnp.max(scores, axis=-1, keepdims=True)
    weights = jnp.exp(scores - row_max)
    weights = (weights / jnp.sum(weights, axis=-1, keepdims=True)).astype(BF16)
    attended = jnp.einsum("nhgqs,nshd->nqhgd", weights, values_split, preferred_element_type=F32)
    attended = attended.reshape(doc_count, length, features).astype(BF16)
    counts = jnp.sum(present.astype(F32), axis=1)
    pooled = (
        jnp.einsum("nt,ntf->nf", present.astype(BF16), attended, preferred_element_type=F32)
        / counts[:, None]
    )
    return attended, pooled


def exclusive_rows(mask):
    size = mask.shape[-1]
    at = jnp.arange(size, dtype=jnp.int32)
    upper = (at[:, None] < at[None, :]).astype(BF16)
    return jnp.dot(mask.astype(BF16), upper, preferred_element_type=F32).astype(jnp.int32)


def routing(codes, flags, me):
    n, docs, length = codes.shape
    place = jnp.arange(docs, dtype=jnp.int32)[None, :] * n + jnp.arange(n, dtype=jnp.int32)[:, None]
    place = place.reshape(-1)
    kept = flags.reshape(-1) == 1
    before = (place[None, :] < place[:, None]) & kept[None, :]
    rank = jnp.where(kept, jnp.sum(before.astype(jnp.int32), axis=1), -1)
    mine = (codes == me).reshape(n * docs, length)
    inner = exclusive_rows(mine)
    count = jnp.sum(mine.astype(jnp.int32), axis=1)
    earlier_rank = jnp.sum(jnp.where(before, count[None, :], 0), axis=1)
    position = earlier_rank[:, None] + inner
    by_source = count.reshape(n, docs)
    doc = jnp.arange(docs, dtype=jnp.int32)
    earlier_doc = jnp.sum(
        jnp.where(doc[None, None, :] < doc[None, :, None], by_source[:, None, :], 0), axis=2
    )
    slot = earlier_doc.reshape(-1)[:, None] + inner
    keys = rank[:, None] * length + jnp.arange(length, dtype=jnp.int32)[None, :]
    return rank, mine, position, slot, keys


def exchange_kernel(
    n, w_ref, rows_ref, docs_ref, info_ref, w_all, rows_all, docs_all, info_all,
    w_send, w_recv, peer_send, peer_recv, own_sem,
):
    me = lax.axis_index("dp")
    planes = n // 4
    plane, spot = lax.div(me, 4), lax.rem(me, 4)
    core, column = lax.rem(spot, 2), lax.div(spot, 2)
    depth = w_ref.shape[0]
    mate = me + 1 - 2 * core
    beside = me + 2 - 4 * column

    barrier = pltpu.get_barrier_semaphore()

    def greet(k, _):
        pl.semaphore_signal(barrier, inc=1, device_id={"dp": lax.rem(me + k, n)}, device_id_type=pl.DeviceIdType.MESH)
        return 0

    lax.fori_loop(1, n, greet, 0)
    pl.semaphore_wait(barrier, n - 1)

    def span(block):
        return pl.ds(pl.multiple_of(block * depth, depth), depth)

    def block_copy(block, lane, target, source=None):
        return pltpu.make_async_remote_copy(
            src_ref=w_all.at[span(block)] if source is None else source,
            dst_ref=w_all.at[span(block)],
            send_sem=w_send.at[lane, block],
            recv_sem=w_recv.at[block],
            device_id={"dp": target},
            device_id_type=pl.DeviceIdType.MESH,
        )

    has_up, has_down = plane < planes - 1, plane > 0

    @pl.when(has_up)
    def _():
        block_copy(me, 0, me + 4, w_ref).start()

    @pl.when(has_down)
    def _():
        block_copy(me, 1, me - 4, w_ref).start()

    block_copy(me, 2, beside, w_ref).start()
    block_copy(me, 3, mate, w_ref).start()

    arrays = ((rows_ref, rows_all), (docs_ref, docs_all), (info_ref, info_all))
    owns = [pltpu.make_async_copy(w_ref, w_all.at[span(me)], own_sem.at[0])]
    owns.append(pltpu.make_async_copy(rows_ref.at[me], rows_all.at[me], own_sem.at[1]))
    owns.append(pltpu.make_async_copy(docs_ref, docs_all.at[me], own_sem.at[2]))
    owns.append(pltpu.make_async_copy(info_ref, info_all.at[me], own_sem.at[3]))
    for copy in owns:
        copy.start()

    def peer_copy(which, k, peer, slot):
        here, there = arrays[which]
        return pltpu.make_async_remote_copy(
            src_ref=here.at[peer] if which == 0 else here,
            dst_ref=there.at[slot],
            send_sem=peer_send.at[which, k],
            recv_sem=peer_recv.at[which, slot],
            device_id={"dp": peer},
            device_id_type=pl.DeviceIdType.MESH,
        )

    def target(k):
        ahead = lax.rem(plane + lax.div(k, 4), planes)
        return ahead * 4 + lax.rem(spot + lax.rem(k, 4), 4)

    def origin(k):
        behind = lax.rem(plane + planes - lax.div(k, 4), planes)
        return behind * 4 + lax.rem(spot + 4 - lax.rem(k, 4), 4)

    def push_small(k, _):
        for which in (2, 1):
            peer_copy(which, k, target(k), me).start()
        return 0

    def push_rows(k, _):
        peer_copy(0, k, target(k), me).start()
        return 0

    lax.fori_loop(1, n, push_small, 0)
    lax.fori_loop(1, 4, push_rows, 0)

    def side_block(block):
        return block + 2 - 4 * column

    def from_side(block):
        block_copy(side_block(block), 3, mate).wait_recv()
        block_copy(side_block(block), 3, mate).start()

    from_side(me)

    def hop(step, _):
        low, high = me - 4 * step, me + 4 * step

        @pl.when(plane - step >= 0)
        def _():
            block_copy(low, 2, beside).wait_recv()

            @pl.when(has_up)
            def _():
                block_copy(low, 0, me + 4).start()

            block_copy(low, 2, beside).start()
            block_copy(low, 3, mate).start()

        @pl.when(plane + step < planes)
        def _():
            block_copy(high, 2, beside).wait_recv()

            @pl.when(has_down)
            def _():
                block_copy(high, 1, me - 4).start()

            block_copy(high, 2, beside).start()
            block_copy(high, 3, mate).start()

        lax.fori_loop(4 * step, 4 * step + 4, push_rows, 0)

        @pl.when(plane - step >= 0)
        def _():
            from_side(low)

        @pl.when(plane + step < planes)
        def _():
            from_side(high)

        return 0

    lax.fori_loop(1, planes, hop, 0)

    def finish(at, _):
        line = at * 4 + spot
        block_copy(line, 2, beside).wait_send()
        block_copy(line, 3, mate).wait_send()
        block_copy(side_block(line), 3, mate).wait_send()
        other = at * 4 + 1 - core
        block_copy(other, 3, mate).wait_recv()
        block_copy(other + 2, 3, mate).wait_recv()

        @pl.when(has_up & (at <= plane))
        def _():
            block_copy(line, 0, me + 4).wait_send()

        @pl.when(has_down & (at >= plane))
        def _():
            block_copy(line, 1, me - 4).wait_send()

        return 0

    lax.fori_loop(0, planes, finish, 0)

    def settle(k, _):
        for which in range(3):
            peer_copy(which, k, target(k), me).wait_send()
            peer_copy(which, k, target(k), origin(k)).wait_recv()
        return 0

    lax.fori_loop(1, n, settle, 0)
    for copy in owns:
        copy.wait()


def exchange(n, weight, rows, docs, info):
    anywhere = pl.BlockSpec(memory_space=pl.ANY)
    shape = jax.ShapeDtypeStruct
    return pl.pallas_call(
        functools.partial(exchange_kernel, n),
        out_shape=(
            shape((n * weight.shape[0], weight.shape[1]), weight.dtype),
            shape(rows.shape, rows.dtype),
            shape((n,) + docs.shape, docs.dtype),
            shape((n,) + info.shape, info.dtype),
        ),
        in_specs=[anywhere] * 4,
        out_specs=(anywhere,) * 4,
        scratch_shapes=[
            pltpu.SemaphoreType.DMA((4, n)),
            pltpu.SemaphoreType.DMA((n,)),
            pltpu.SemaphoreType.DMA((3, n)),
            pltpu.SemaphoreType.DMA((3, n)),
            pltpu.SemaphoreType.DMA((4,)),
        ],
        compiler_params=pltpu.CompilerParams(collective_id=0, has_side_effects=True),
    )(weight, rows, docs, info)


def place_kernel(position_ref, arrived_ref, docs_ref, w_ref, out_ref, docs_out_ref):
    tile = out_ref.shape[0]
    row = lax.broadcasted_iota(jnp.int32, (tile, position_ref.shape[1]), 0) + pl.program_id(0) * tile
    order = jnp.where(row == position_ref[...], 1.0, 0.0).astype(BF16)
    chosen = jnp.dot(order, arrived_ref[...], preferred_element_type=F32).astype(BF16)
    both = jnp.concatenate([chosen, docs_ref[...]], axis=0)
    unit = normalize(jnp.dot(both, w_ref[...], preferred_element_type=F32))
    out_ref[...] = unit[:tile]
    docs_out_ref[...] = unit[tile:]


def place(rows, positions, arrived, doc_rows, weight):
    width = weight.shape[1]
    tile = min(rows, 256)
    whole = lambda array: pl.BlockSpec(array.shape, lambda i: (0, 0))
    return pl.pallas_call(
        place_kernel,
        grid=(rows // tile,),
        out_shape=(
            jax.ShapeDtypeStruct((rows, width), BF16),
            jax.ShapeDtypeStruct((doc_rows.shape[0], width), BF16),
        ),
        in_specs=[whole(positions), whole(arrived), whole(doc_rows), whole(weight)],
        out_specs=(
            pl.BlockSpec((tile, width), lambda i: (i, 0)),
            pl.BlockSpec((doc_rows.shape[0], width), lambda i: (0, 0)),
        ),
        compiler_params=pltpu.CompilerParams(vmem_limit_bytes=50 * 2**20),
    )(positions, arrived, doc_rows, weight)


def shards(
    query_states, key_states, value_states, out_weight, token_ids, keep_flags, list_ids, owner_map
):
    n = lax.axis_size("dp")
    me = lax.axis_index("dp").astype(jnp.int32)
    docs, length, features = query_states.shape
    rows = docs * length
    cap = -(-3 * rows // (2 * n) // 16) * 16

    lists = owner_map.shape[0]
    hit = list_ids.reshape(-1)[:, None] == jnp.arange(lists, dtype=jnp.int32)[None, :]
    owners = jnp.sum(jnp.where(hit, owner_map[None, :], 0), axis=1).reshape(docs, length)
    codes = jnp.where((keep_flags == 1)[:, None] & (token_ids != 0), owners, -1)
    info = jnp.concatenate([codes, jnp.broadcast_to(keep_flags[:, None], (docs, length))], axis=0)
    flat = codes.reshape(-1)
    member = (flat[None, :] == jnp.arange(n, dtype=jnp.int32)[:, None])
    at = jnp.arange(rows, dtype=jnp.int32)
    tri = (at[:, None] < at[None, :]).astype(BF16)
    within = jnp.dot(member.astype(BF16), tri, preferred_element_type=F32).astype(jnp.int32)
    pick = (
        member[:, None, :]
        & (within[:, None, :] == jnp.arange(cap, dtype=jnp.int32)[None, :, None])
    ).astype(BF16).reshape(n * cap, rows)

    attended, pooled = attend(query_states, key_states, value_states, token_ids)
    packed = jnp.dot(pick, attended.reshape(rows, features), preferred_element_type=F32).astype(BF16)
    sent_docs = pooled.astype(BF16).reshape(16, docs * features // 16)
    weight, arrived, every_doc, every = exchange(
        n, out_weight, packed.reshape(n, cap, features), sent_docs, info
    )
    arrived = arrived.reshape(n * cap, features)
    every_doc = every_doc.reshape(n * docs, features)
    rank, mine, position, slot, keys = routing(every[:, :docs], every[:, docs:, 0], me)

    mine_s = mine.reshape(n, rows)
    slot_s = jnp.where(mine_s, slot.reshape(n, rows), -1)
    fits = slot_s[:, None, :] == jnp.arange(cap, dtype=jnp.int32)[None, :, None]
    slot_position = jnp.sum(
        jnp.where(fits, position.reshape(n, 1, rows) + 1, 0), axis=2
    ).reshape(-1) - 1
    slot_key = jnp.sum(jnp.where(fits, keys.reshape(n, 1, rows) + 1, 0), axis=2).reshape(-1)
    order = jnp.arange(rows, dtype=jnp.int32)[:, None] == slot_position[None, :]
    token_keys = jnp.sum(jnp.where(order, slot_key[None, :], 0), axis=1) - 1
    kept_slots = 3 * docs // 4
    held = -(-kept_slots // 16) * 16
    slots = jnp.arange(held, dtype=jnp.int32)
    wanted = jnp.where(slots < kept_slots, slots * n + me, n * docs)
    picker = (rank[None, :] == wanted[:, None]).astype(BF16)
    chosen = jnp.dot(picker, every_doc, preferred_element_type=F32).astype(BF16)
    token_vectors, unit_docs = place(rows, slot_position[None, :], arrived, chosen, weight)
    doc_vectors = unit_docs[:kept_slots]
    return (doc_vectors, token_vectors, token_keys)


def solution(mesh):
    return jax.shard_map(
        shards,
        mesh=mesh,
        in_specs=(
            P(("groups", "dp"), None, None),
            P(("groups", "dp"), None, None),
            P(("groups", "dp"), None, None),
            P("dp", None),
            P(("groups", "dp"), None),
            P(("groups", "dp")),
            P(("groups", "dp"), None),
            P("groups"),
        ),
        out_specs=(P(("groups", "dp"), None), P(("groups", "dp"), None), P(("groups", "dp"))),
        check_vma=False,
    )
```
